256 devices in a mesh: rows: 16 (over z, core), cols: 16 (over y, x).
Axes of the slice: x: 4, y: 4, z: 8, core: 2. Of those that a mesh axis runs over, the one named last changes fastest.
Arguments:
- embeddings: float32 [262144, 1024], P(('rows', 'cols')), may hold values from -70 to 70
Outputs:
- whitened: float32 [262144, 1024], P(('rows', 'cols'))
The draws below stay inside these ranges and needn't reach their ends.
All inputs are finite; a program needn't handle non-finite values.
Results may differ from the reference program's by a relative error of at most 0.000057.
Values sent between devices are 32-bit elements; how exact they have to be, the bound alone decides.
No kernel may reach another device: no remote copies, remote signals or barrier semaphores. Data moves between devices by JAX's collectives and lax.ppermute only.
A program may use at most 128 MiB of HBM per device.

```python
import math
import jax
import jax.numpy as jnp
from jax import lax

D = 1024
ROWS = 262144


def draw_embeddings(key, part):
    key = jax.random.fold_in(key, 11)
    keys = jax.random.split(key, 6)
    noise = jnp.clip(jax.random.normal(keys[0], (ROWS, D), jnp.float32), -4.0, 4.0)
    strength = 0.3
    offset = 1.0
    column_scale = jnp.exp(jax.random.uniform(keys[1], (1, D), jnp.float32, 0.0, 0.6931))
    row_weight = jnp.clip(jax.random.normal(keys[2], (ROWS, 1), jnp.float32), -4.0, 4.0)
    direction = jnp.clip(jax.random.normal(keys[3], (1, D), jnp.float32), -4.0, 4.0)
    shift = jax.random.uniform(keys[4], (1, D), jnp.float32, -offset, offset)
    position = jnp.arange(ROWS, dtype=jnp.float32).reshape(ROWS, 1) / ROWS
    row_scale = (1.0 + 2.0 * position) * jnp.exp(jax.random.uniform(keys[5], (ROWS, 1), jnp.float32, -0.3, 0.3))
    values = row_scale * (noise * column_scale + strength * row_weight * direction + shift)
    return values.astype(jnp.float32)


def setup_inputs(seed: int = 0) -> dict:
    splits = jax.random.split(jax.random.key(seed), 2)
    embeddings = draw_embeddings(jax.random.fold_in(splits[1], 71), 0)
    return dict(embeddings=embeddings)


def reference(embeddings):
    row_count = embeddings.shape[0]
    column_mean = lax.optimization_barrier(jnp.sum(embeddings, axis=0)) / jnp.float32(row_count)
    centered = embeddings - column_mean
    covariance = lax.dot_general(centered.astype(jnp.float32), centered.astype(jnp.float32), (((0,), (0,)), ((), ())), precision=lax.Precision.HIGHEST, preferred_element_type=jnp.float32)
    factor = jnp.linalg.cholesky(covariance)
    solved = lax.linalg.triangular_solve(factor, centered, left_side=False, lower=True, transpose_a=True)
    return solved * jnp.float32(math.sqrt(row_count))
```

```python
import functools
import math

import jax
import jax.numpy as jnp
from jax import lax
from jax.experimental import pallas as pl
from jax.experimental.pallas import tpu as pltpu
from jax.sharding import Mesh, PartitionSpec as P

B = 128
HIGHEST = lax.Precision.HIGHEST
NB = 8
LOWER = [(i, j) for i in range(NB) for j in range(i)]
PAIRS = [(2 * s, 2 * s + 1) for s in range(NB // 2)]
CHUNKS = len(LOWER) + len(PAIRS)
HALF = CHUNKS // 2
ROWS = B + 8
VMEM = pl.BlockSpec(memory_space=pltpu.VMEM)
SMEM = pl.BlockSpec(memory_space=pltpu.SMEM)
PARAMS = pltpu.CompilerParams(vmem_limit_bytes=56 * 1024 * 1024)


def dot(a, b, dims):
    return lax.dot_general(a, b, ((dims[0:1], dims[1:2]), ((), ())), precision=HIGHEST, preferred_element_type=jnp.float32)


def iota(shape, axis):
    return lax.broadcasted_iota(jnp.int32, shape, axis)


def gram_kernel(core_ref, x_ref, keep_ref, send_ref, mean_ref, xc_ref):
    n, d = x_ref.shape
    mean = jnp.sum(x_ref[...], axis=0, keepdims=True) * (1.0 / n)
    xc_ref[...] = x_ref[...] - mean
    core = core_ref[0]
    lower = iota((B, B), 0) >= iota((B, B), 1)

    def put(chunk, block, tile):
        def write(ref):
            ref[chunk % HALF, 0:B, :] = block
            ref[chunk % HALF, B:, :] = tile

        mine = core == chunk // HALF

        @pl.when(mine)
        def _():
            write(keep_ref)

        @pl.when(jnp.logical_not(mine))
        def _():
            write(send_ref)

    def seg(i):
        return mean[:, B * i : B * i + B]

    zero = jnp.zeros((1, B), jnp.float32)
    for bi in range(NB // 2):
        for bj in range(bi + 1):
            g = dot(xc_ref[:, 2 * B * bi : 2 * B * bi + 2 * B], xc_ref[:, 2 * B * bj : 2 * B * bj + 2 * B], (0, 0))
            for u in range(2):
                for v in range(2):
                    i, j = 2 * bi + u, 2 * bj + v
                    if i > j:
                        tile = jnp.concatenate([seg(i), seg(j), seg(i), seg(j), zero, zero, zero, zero], axis=0)
                        put(LOWER.index((i, j)), g[B * u : B * u + B, B * v : B * v + B], tile)
            if bi == bj:
                first, second = g[0:B, 0:B], g[B:, B:]
                diag = jnp.sum(jnp.where(iota((B, B), 0) == iota((B, B), 1), second, 0.0), axis=0, keepdims=True)
                i, j = 2 * bi, 2 * bi + 1
                tile = jnp.concatenate([seg(i), seg(i), seg(j), seg(j), diag, zero, zero, zero], axis=0)
                put(len(LOWER) + bi, jnp.where(lower, first, second), tile)


def local_gram(x, core):
    shape = jax.ShapeDtypeStruct((HALF, ROWS, B), jnp.float32)
    return pl.pallas_call(
        gram_kernel,
        out_shape=(shape, shape),
        in_specs=[SMEM, VMEM],
        out_specs=(VMEM, VMEM),
        scratch_shapes=[pltpu.VMEM((1, x.shape[1]), jnp.float32), pltpu.VMEM(x.shape, jnp.float32)],
        compiler_params=PARAMS,
    )(core, x)


def merge(parts, count):
    k = len(parts)
    block, tile = parts[0]
    for b, t in parts[1:]:
        block = block + b
        tile = tile + t
    mean = tile * (1.0 / k)
    sub = iota((8, B), 0)
    left, right = [], []
    square = jnp.zeros((8, B), jnp.float32)
    for _, t in parts:
        delta = jnp.where(sub < 4, t - mean, 0.0)
        moved = jnp.concatenate([delta[1:8], delta[0:1]], axis=0)
        left.append(delta)
        right.append(moved)
        square = square + delta * delta
    left = jnp.concatenate(left, axis=0)
    right = jnp.concatenate(right, axis=0)
    row = iota(left.shape, 0) % 8
    low = dot(jnp.where(row == 0, left, 0.0), jnp.where(row == 0, right, 0.0), (0, 0))
    high = dot(jnp.where(row == 2, left, 0.0), jnp.where(row == 2, right, 0.0), (0, 0))
    lower = iota((B, B), 0) >= iota((B, B), 1)
    block = block + count * jnp.where(lower, low, high)
    diag = tile[4:5] + count * square[2:3]
    tile = jnp.where(sub < 4, mean, jnp.where(sub == 4, jnp.broadcast_to(diag, (8, B)), 0.0))
    return block, tile


def pair_kernel(count, a_ref, b_ref, o_ref):
    for c in range(a_ref.shape[0]):
        block, tile = merge([(r[c, 0:B, :], r[c, B:, :]) for r in (a_ref, b_ref)], count)
        o_ref[c, 0:B, :] = block
        o_ref[c, B:, :] = tile


def merge_pair(a, b, count):
    return pl.pallas_call(
        functools.partial(pair_kernel, float(count)),
        out_shape=jax.ShapeDtypeStruct(a.shape, jnp.float32),
        in_specs=[VMEM, VMEM],
        out_specs=VMEM,
        compiler_params=PARAMS,
    )(a, b)


def many_kernel(count, a_ref, o_ref):
    block, tile = merge([(a_ref[c, 0:B, :], a_ref[c, B:, :]) for c in range(a_ref.shape[0])], count)
    o_ref[0, 0:B, :] = block
    o_ref[0, B:, :] = tile


def merge_many(a, count):
    return pl.pallas_call(
        functools.partial(many_kernel, float(count)),
        out_shape=jax.ShapeDtypeStruct((1,) + a.shape[1:], jnp.float32),
        in_specs=[VMEM],
        out_specs=VMEM,
        compiler_params=PARAMS,
    )(a)


def row_of(x, j):
    return jnp.broadcast_to(x[j : j + 1, :], x.shape)


def column_of(x, j):
    return jnp.broadcast_to(x[:, j : j + 1], x.shape)


def factor_inverse(rows):
    rows = list(rows)
    sub, lane = iota((8, B), 0), iota((8, B), 1)
    for p in range(len(rows)):
        own = (lane >= 8 * p) & (lane < 8 * p + 8)
        cols = {q: [column_of(rows[q], 8 * p + j) for j in range(8)] for q in range(p, len(rows))}
        rows[p] = jnp.where(own, (lane - 8 * p == sub).astype(jnp.float32), rows[p])
        for q in range(p + 1, len(rows)):
            rows[q] = jnp.where(own, 0.0, rows[q])
        pivots = None
        for j in range(8):
            pivot = row_of(cols[p][j], j)
            pivots = pivot if j == 0 else jnp.where(sub == j, pivot, pivots)
            inverse = pl.reciprocal(pivot, approx=False)
            heads = {m: row_of(cols[p][m], j) for m in range(j + 1, 8)}
            head = row_of(rows[p], j)
            for q in range(p, len(rows)):
                coef = cols[q][j] * inverse
                if q == p:
                    coef = jnp.where(sub > j, coef, 0.0)
                for m in range(j + 1, 8):
                    cols[q][m] = cols[q][m] - coef * heads[m]
                rows[q] = rows[q] - coef * head
        rows[p] = rows[p] * lax.rsqrt(pivots)
    return rows


def solve_kernel(scale, core_ref, x_ref, own_ref, other_ref, y_ref, a_ref, z_ref, w_ref, l_ref):
    core = core_ref[0]
    lower = iota((B, B), 0) > iota((B, B), 1)
    equal = iota((B, B), 0) == iota((B, B), 1)
    n, d = x_ref.shape

    def chunk(c, lo, hi):
        mine = core == c // HALF
        return jnp.where(mine, own_ref[c % HALF, lo:hi, :], other_ref[c % HALF, lo:hi, :])

    means = []
    for s in range(len(PAIRS)):
        block = chunk(len(LOWER) + s, 0, B)
        tile = chunk(len(LOWER) + s, B, ROWS)
        means += [tile[0:1, :], tile[2:3, :]]
        low = jnp.where(lower, block, 0.0)
        first = jnp.where(equal, block, low + low.T)
        high = jnp.where(lower | equal, 0.0, block)
        second = jnp.where(equal, jnp.broadcast_to(tile[4:5, :], (B, B)), high + high.T)
        for i, value in ((2 * s, first), (2 * s + 1, second)):
            a_ref[B * i : B * i + B, B * i : B * i + B] = value
    for c, (i, j) in enumerate(LOWER):
        a_ref[B * i : B * i + B, B * j : B * j + B] = chunk(c, 0, B)
    mean = jnp.concatenate(means, axis=1)
    z_ref[...] = (x_ref[...] - mean) * scale

    for k in range(NB):
        lo, hi = B * k, B * k + B
        rows = factor_inverse([a_ref[lo + 8 * p : lo + 8 * p + 8, lo:hi] for p in range(B // 8)])
        for p, r in enumerate(rows):
            w_ref[8 * p : 8 * p + 8, :] = r
        w = jnp.where(lower | equal, w_ref[...], 0.0)
        if k + 1 < NB:
            l_ref[hi:d, :] = dot(a_ref[hi:d, lo:hi], w, (1, 1))
            for j in range(k + 1, NB):
                jl, jh = B * j, B * j + B
                a_ref[jl:d, jl:jh] = a_ref[jl:d, jl:jh] - dot(l_ref[jl:d, :], l_ref[jl:jh, :], (1, 1))
        y = dot(z_ref[:, lo:hi], w, (1, 1))
        y_ref[:, lo:hi] = y
        if k + 1 < NB:
            z_ref[:, hi:d] = z_ref[:, hi:d] - dot(y, l_ref[hi:d, :], (1, 1))


def factor_solve(x, own, other, core, scale):
    return pl.pallas_call(
        functools.partial(solve_kernel, scale),
        out_shape=jax.ShapeDtypeStruct(x.shape, jnp.float32),
        in_specs=[SMEM, VMEM, VMEM, VMEM],
        out_specs=VMEM,
        scratch_shapes=[
            pltpu.VMEM((x.shape[1], x.shape[1]), jnp.float32),
            pltpu.VMEM(x.shape, jnp.float32),
            pltpu.VMEM((B, B), jnp.float32),
            pltpu.VMEM((x.shape[1], B), jnp.float32),
        ],
        compiler_params=PARAMS,
    )(core, x, own, other)


def z_steps():
    gray = [i ^ (i >> 1) for i in range(8)]
    place = {g: i for i, g in enumerate(gray)}
    return [[(i, place[gray[i] ^ (1 << k)]) for i in range(8)] for k in range(3)]


def per_device(x):
    n = x.shape[0]
    total = n * lax.axis_size("z") * lax.axis_size("core") * lax.axis_size("cols")
    core = jnp.reshape(lax.axis_index("core"), (1,)).astype(jnp.int32)
    swap = [(0, 1), (1, 0)]
    keep, send = local_gram(x, core)
    part = merge_pair(keep, lax.ppermute(send, "core", swap), n)
    part = lax.all_to_all(part, "cols", 0, 0, tiled=True)
    part = merge_many(part, 2 * n)
    count = 2 * n * lax.axis_size("cols")
    for step in z_steps():
        part = merge_pair(part, lax.ppermute(part, "z", step), count)
        count = 2 * count
    copies = jnp.broadcast_to(part, (HALF,) + part.shape[1:])
    own = lax.all_to_all(copies, "cols", 0, 0, tiled=True)
    other = lax.ppermute(own, "core", swap)
    return factor_solve(x, own, other, core, math.sqrt(total))


def solution(mesh):
    rows, cols = mesh.devices.shape
    fine = Mesh(mesh.devices.reshape(rows // 2, 2, cols), ("z", "core", "cols"))
    spec = P(("z", "core", "cols"), None)
    return jax.shard_map(per_device, mesh=fine, in_specs=(spec,), out_specs=spec, check_vma=False)
```

```python
import functools
import math

import jax
import jax.numpy as jnp
from jax import lax
from jax.experimental import pallas as pl
from jax.experimental.pallas import tpu as pltpu
from jax.sharding import Mesh, PartitionSpec as P

B = 128
STEP = 256
HIGHEST = lax.Precision.HIGHEST
NB = 8
LOWER = [(i, j) for i in range(NB) for j in range(i)]
PAIRS = [(2 * s, 2 * s + 1) for s in range(NB // 2)]
CHUNKS = len(LOWER) + len(PAIRS)
HALF = CHUNKS // 2
ROWS = B + 8
VMEM = pl.BlockSpec(memory_space=pltpu.VMEM)
SMEM = pl.BlockSpec(memory_space=pltpu.SMEM)
PARAMS = pltpu.CompilerParams(vmem_limit_bytes=56 * 1024 * 1024)


def dot(a, b, dims):
    return lax.dot_general(a, b, ((dims[0:1], dims[1:2]), ((), ())), precision=HIGHEST, preferred_element_type=jnp.float32)


def iota(shape, axis):
    return lax.broadcasted_iota(jnp.int32, shape, axis)


def gram_kernel(core_ref, x_ref, keep_ref, send_ref, hi_ref, mid_ref, hit_ref, midt_ref):
    n, d = x_ref.shape
    wide = 2 * B
    mean = jnp.concatenate(
        [jnp.sum(x_ref[:, c : c + B], axis=0, keepdims=True) * (1.0 / n) for c in range(0, d, B)], axis=1
    )

    squares = []

    def prepare(i):
        c = wide * i
        xc = x_ref[:, c : c + wide] - mean[:, c : c + wide]
        hi = xc.astype(jnp.bfloat16)
        mid = (xc - hi.astype(jnp.float32)).astype(jnp.bfloat16)
        hi_ref[:, c : c + wide] = hi
        mid_ref[:, c : c + wide] = mid
        low = mid.astype(jnp.float32)
        squares.append(jnp.sum(low * low, axis=0, keepdims=True))
        xt = xc.T
        hi = xt.astype(jnp.bfloat16)
        hit_ref[c : c + wide, :] = hi
        midt_ref[c : c + wide, :] = (xt - hi.astype(jnp.float32)).astype(jnp.bfloat16)

    def product(j):
        total = None
        for a, b in ((hit_ref, hi_ref), (hit_ref, mid_ref), (midt_ref, hi_ref)):
            part = jnp.dot(a[wide * j : d, :], b[:, wide * j : wide * j + wide], preferred_element_type=jnp.float32)
            total = part if total is None else total + part
        return total

    core = core_ref[0]
    lower = iota((B, B), 0) >= iota((B, B), 1)

    def put(chunk, block, tile):
        def write(ref):
            ref[chunk % HALF, 0:B, :] = block
            ref[chunk % HALF, B:, :] = tile

        mine = core == chunk // HALF

        @pl.when(mine)
        def _():
            write(keep_ref)

        @pl.when(jnp.logical_not(mine))
        def _():
            write(send_ref)

    def seg(i):
        return mean[:, B * i : B * i + B]

    zero = jnp.zeros((1, B), jnp.float32)
    for bi in range(NB // 2):
        prepare(bi)
    for bj in range(NB // 2):
        panel = product(bj)
        for bi in range(bj, NB // 2):
            g = panel[wide * (bi - bj) : wide * (bi - bj) + wide, :]
            for u in range(2):
                for v in range(2):
                    i, j = 2 * bi + u, 2 * bj + v
                    if i > j:
                        tile = jnp.concatenate([seg(i), seg(j), seg(i), seg(j), zero, zero, zero, zero], axis=0)
                        put(LOWER.index((i, j)), g[B * u : B * u + B, B * v : B * v + B], tile)
            if bi == bj:
                on = iota((B, B), 0) == iota((B, B), 1)
                first = g[0:B, 0:B] + jnp.where(on, squares[bi][:, 0:B], 0.0)
                second = g[B:, B:] + jnp.where(on, squares[bi][:, B:], 0.0)
                diag = jnp.sum(jnp.where(on, second, 0.0), axis=0, keepdims=True)
                i, j = 2 * bi, 2 * bi + 1
                tile = jnp.concatenate([seg(i), seg(i), seg(j), seg(j), diag, zero, zero, zero], axis=0)
                put(len(LOWER) + bi, jnp.where(lower, first, second), tile)


def local_gram(x, core):
    shape = jax.ShapeDtypeStruct((HALF, ROWS, B), jnp.float32)
    return pl.pallas_call(
        gram_kernel,
        out_shape=(shape, shape),
        in_specs=[SMEM, VMEM],
        out_specs=(VMEM, VMEM),
        scratch_shapes=[pltpu.VMEM(x.shape, jnp.bfloat16)] * 4,
        compiler_params=PARAMS,
    )(core, x)


def merge_kernel(count, a_ref, o_ref):
    sources, rows, _ = a_ref.shape
    block = a_ref[0, 0:B, :]
    for c in range(1, sources):
        block = block + a_ref[c, 0:B, :]
    tiles = [a_ref[c, t : t + 8, :] for c in range(sources) for t in range(B, rows, 8)]
    total = tiles[0]
    for t in tiles[1:]:
        total = total + t
    mean = total * (1.0 / len(tiles))
    sub = iota((8, B), 0)
    left, right = [], []
    square = jnp.zeros((8, B), jnp.float32)
    for t in tiles:
        delta = jnp.where(sub < 4, t - mean, 0.0)
        left.append(delta)
        right.append(jnp.concatenate([delta[1:8], delta[0:1]], axis=0))
        square = square + delta * delta
    left = jnp.concatenate(left, axis=0)
    right = jnp.concatenate(right, axis=0)
    row = iota(left.shape, 0) % 8
    low = dot(jnp.where(row == 0, left, 0.0), jnp.where(row == 0, right, 0.0), (0, 0))
    high = dot(jnp.where(row == 2, left, 0.0), jnp.where(row == 2, right, 0.0), (0, 0))
    lower = iota((B, B), 0) >= iota((B, B), 1)
    block = block + count * jnp.where(lower, low, high)
    diag = total[4:5] + count * square[2:3]
    tile = jnp.where(sub < 4, mean, jnp.where(sub == 4, jnp.broadcast_to(diag, (8, B)), 0.0))
    for c in range(o_ref.shape[0]):
        o_ref[c, 0:B, :] = block
        o_ref[c, B:, :] = tile


def merge(a, count, copies):
    return pl.pallas_call(
        functools.partial(merge_kernel, float(count)),
        out_shape=jax.ShapeDtypeStruct((copies, ROWS, B), jnp.float32),
        in_specs=[VMEM],
        out_specs=VMEM,
        compiler_params=PARAMS,
    )(a)


def join(a, b):
    return jnp.concatenate([a[:, 0:B] + b[:, 0:B], a[:, B:], b[:, B:]], axis=1)


def row_of(x, j):
    return jnp.broadcast_to(x[j : j + 1, :], x.shape)


def column_of(x, j):
    return jnp.broadcast_to(x[:, j : j + 1], x.shape)


def factor_inverse(rows):
    sub, lane = iota((8, B), 0), iota((8, B), 1)
    for p in range(len(rows)):
        own = (lane >= 8 * p) & (lane < 8 * p + 8)
        cols = {q: [column_of(rows[q], 8 * p + j) for j in range(8)] for q in range(p, len(rows))}
        rows[p] = jnp.where(own, (lane - 8 * p == sub).astype(jnp.float32), rows[p])
        for q in range(p + 1, len(rows)):
            rows[q] = jnp.where(own, 0.0, rows[q])
        pivots = None
        for j in range(8):
            pivot = row_of(cols[p][j], j)
            pivots = pivot if j == 0 else jnp.where(sub == j, pivot, pivots)
            inverse = pl.reciprocal(pivot, approx=False)
            heads = {m: row_of(cols[p][m], j) for m in range(j + 1, 8)}
            head = row_of(rows[p], j)
            for q in range(p, len(rows)):
                coef = cols[q][j] * inverse
                if q == p:
                    coef = jnp.where(sub > j, coef, 0.0)
                for m in range(j + 1, 8):
                    cols[q][m] = cols[q][m] - coef * heads[m]
                rows[q] = rows[q] - coef * head
        rows[p] = rows[p] * lax.rsqrt(pivots)
        yield p


def solve_kernel(scale, core_ref, x_ref, own_ref, other_ref, y_ref, a_ref, z_ref, w_ref, l_ref):
    core = core_ref[0]
    lower = iota((B, B), 0) > iota((B, B), 1)
    equal = iota((B, B), 0) == iota((B, B), 1)
    n, d = x_ref.shape

    def chunk(c, lo, hi):
        mine = core == c // HALF
        return jnp.where(mine, own_ref[c % HALF, lo:hi, :], other_ref[c % HALF, lo:hi, :])

    means = []
    for s in range(len(PAIRS)):
        block = chunk(len(LOWER) + s, 0, B)
        tile = chunk(len(LOWER) + s, B, ROWS)
        means += [tile[0:1, :], tile[2:3, :]]
        low = jnp.where(lower, block, 0.0)
        first = jnp.where(equal, block, low + low.T)
        high = jnp.where(lower | equal, 0.0, block)
        second = jnp.where(equal, jnp.broadcast_to(tile[4:5, :], (B, B)), high + high.T)
        for i, value in ((2 * s, first), (2 * s + 1, second)):
            a_ref[B * i : B * i + B, B * i : B * i + B] = value
    for c, (i, j) in enumerate(LOWER):
        a_ref[B * i : B * i + B, B * j : B * j + B] = chunk(c, 0, B)
    mean = jnp.concatenate(means, axis=1)
    z_ref[...] = (x_ref[...] - mean) * scale

    later = []
    head = a_ref[0:B, 0:B]
    for k in range(NB):
        lo, hi = B * k, B * k + B
        rows = [head[8 * p : 8 * p + 8, :] for p in range(B // 8)]
        per = -(-len(later) // (B // 8))
        for p in factor_inverse(rows):
            for task in later[per * p : per * p + per]:
                task()
        later = []
        w = jnp.where(lower | equal, jnp.concatenate(rows, axis=0), 0.0)
        if k + 1 < NB:
            near = dot(a_ref[hi : hi + B, lo:hi], w, (1, 1))
            head = a_ref[hi : hi + B, hi : hi + B] - dot(near, near, (1, 1))
            l_ref[k % 2, hi : hi + B, :] = near
            if k + 2 < NB:
                l_ref[k % 2, hi + B : d, :] = dot(a_ref[hi + B : d, lo:hi], w, (1, 1))
        w_ref[k % 2] = w

        def update(j, k=k):
            jl, jh = B * j, B * j + B
            a_ref[jl:d, jl:jh] = a_ref[jl:d, jl:jh] - dot(l_ref[k % 2, jl:d, :], l_ref[k % 2, jl:jh, :], (1, 1))

        def first(k=k):
            jl, jh = B * k + B, B * k + 2 * B
            l = l_ref[k % 2]
            a_ref[jh:d, jl:jh] = a_ref[jh:d, jl:jh] - dot(l[jh:d, :], l[jl:jh, :], (1, 1))

        def solved(r, k=k):
            lo, hi = B * k, B * k + B
            y_ref[r : r + STEP, lo:hi] = dot(z_ref[r : r + STEP, lo:hi], w_ref[k % 2], (1, 1))

        def reduced(r, k=k):
            lo, hi = B * k, B * k + B
            z_ref[r : r + STEP, hi:d] = z_ref[r : r + STEP, hi:d] - dot(
                y_ref[r : r + STEP, lo:hi], l_ref[k % 2, hi:d, :], (1, 1)
            )

        if k + 2 < NB:
            later.append(first)
        later += [functools.partial(update, j) for j in range(k + 2, NB)]
        later += [functools.partial(solved, r) for r in range(0, n, STEP)]
        if k + 1 < NB:
            later += [functools.partial(reduced, r) for r in range(0, n, STEP)]
    for task in later:
        task()


def factor_solve(x, own, other, core, scale):
    return pl.pallas_call(
        functools.partial(solve_kernel, scale),
        out_shape=jax.ShapeDtypeStruct(x.shape, jnp.float32),
        in_specs=[SMEM, VMEM, VMEM, VMEM],
        out_specs=VMEM,
        scratch_shapes=[
            pltpu.VMEM((x.shape[1], x.shape[1]), jnp.float32),
            pltpu.VMEM(x.shape, jnp.float32),
            pltpu.VMEM((2, B, B), jnp.float32),
            pltpu.VMEM((2, x.shape[1], B), jnp.float32),
        ],
        compiler_params=PARAMS,
    )(core, x, own, other)


def z_steps():
    gray = [i ^ (i >> 1) for i in range(8)]
    place = {g: i for i, g in enumerate(gray)}
    return [[(i, place[gray[i] ^ (1 << k)]) for i in range(8)] for k in range(3)]


def per_device(x):
    n = x.shape[0]
    total = n * lax.axis_size("z") * lax.axis_size("core") * lax.axis_size("cols")
    core = jnp.reshape(lax.axis_index("core"), (1,)).astype(jnp.int32)
    swap = [(0, 1), (1, 0)]
    keep, send = local_gram(x, core)
    part = join(keep, lax.ppermute(send, "core", swap))
    part = lax.all_to_all(part, "cols", 0, 0, tiled=True)
    part = merge(part, n, 1)
    for step in z_steps():
        part = join(part, lax.ppermute(part, "z", step))
    copies = merge(part, 2 * n * lax.axis_size("cols"), HALF)
    own = lax.all_to_all(copies, "cols", 0, 0, tiled=True)
    other = lax.ppermute(own, "core", swap)
    return factor_solve(x, own, other, core, math.sqrt(total))


def solution(mesh):
    rows, cols = mesh.devices.shape
    fine = Mesh(mesh.devices.reshape(rows // 2, 2, cols), ("z", "core", "cols"))
    spec = P(("z", "core", "cols"), None)
    return jax.shard_map(per_device, mesh=fine, in_specs=(spec,), out_specs=spec, check_vma=False)
```

```python
import functools
import math

import jax
import jax.numpy as jnp
from jax import lax
from jax.experimental import pallas as pl
from jax.experimental.pallas import tpu as pltpu
from jax.sharding import Mesh, PartitionSpec as P

B = 128
STEP = 256
HIGHEST = lax.Precision.HIGHEST
NB = 8
LOWER = [(i, j) for i in range(NB) for j in range(i)]
PAIRS = [(2 * s, 2 * s + 1) for s in range(NB // 2)]
CHUNKS = len(LOWER) + len(PAIRS)
HALF = CHUNKS // 2
ROWS = B + 8
VMEM = pl.BlockSpec(memory_space=pltpu.VMEM)
SMEM = pl.BlockSpec(memory_space=pltpu.SMEM)
PARAMS = pltpu.CompilerParams(vmem_limit_bytes=56 * 1024 * 1024)


def dot(a, b, dims):
    return lax.dot_general(a, b, ((dims[0:1], dims[1:2]), ((), ())), precision=HIGHEST, preferred_element_type=jnp.float32)


def iota(shape, axis):
    return lax.broadcasted_iota(jnp.int32, shape, axis)


def gram_kernel(core_ref, x_ref, keep_ref, send_ref, hi_ref, mid_ref, hit_ref, midt_ref):
    n, d = x_ref.shape
    wide = 2 * B
    mean = jnp.concatenate(
        [jnp.sum(x_ref[:, c : c + B], axis=0, keepdims=True) * (1.0 / n) for c in range(0, d, B)], axis=1
    )

    squares = []

    def prepare(i):
        c = wide * i
        xc = x_ref[:, c : c + wide] - mean[:, c : c + wide]
        hi = xc.astype(jnp.bfloat16)
        mid = (xc - hi.astype(jnp.float32)).astype(jnp.bfloat16)
        hi_ref[:, c : c + wide] = hi
        mid_ref[:, c : c + wide] = mid
        low = mid.astype(jnp.float32)
        squares.append(jnp.sum(low * low, axis=0, keepdims=True))
        xt = xc.T
        hi = xt.astype(jnp.bfloat16)
        hit_ref[c : c + wide, :] = hi
        midt_ref[c : c + wide, :] = (xt - hi.astype(jnp.float32)).astype(jnp.bfloat16)

    def product(j):
        total = None
        for a, b in ((hit_ref, hi_ref), (hit_ref, mid_ref), (midt_ref, hi_ref)):
            part = jnp.dot(a[wide * j : d, :], b[:, wide * j : wide * j + wide], preferred_element_type=jnp.float32)
            total = part if total is None else total + part
        return total

    core = core_ref[0]
    lower = iota((B, B), 0) >= iota((B, B), 1)

    def put(chunk, block, tile):
        def write(ref):
            ref[chunk % HALF, 0:B, :] = block
            ref[chunk % HALF, B:, :] = tile

        mine = core == chunk // HALF

        @pl.when(mine)
        def _():
            write(keep_ref)

        @pl.when(jnp.logical_not(mine))
        def _():
            write(send_ref)

    def seg(i):
        return mean[:, B * i : B * i + B]

    zero = jnp.zeros((1, B), jnp.float32)
    for bi in range(NB // 2):
        prepare(bi)
    for bj in range(NB // 2):
        panel = product(bj)
        for bi in range(bj, NB // 2):
            g = panel[wide * (bi - bj) : wide * (bi - bj) + wide, :]
            for u in range(2):
                for v in range(2):
                    i, j = 2 * bi + u, 2 * bj + v
                    if i > j:
                        tile = jnp.concatenate([seg(i), seg(j), seg(i), seg(j), zero, zero, zero, zero], axis=0)
                        put(LOWER.index((i, j)), g[B * u : B * u + B, B * v : B * v + B], tile)
            if bi == bj:
                on = iota((B, B), 0) == iota((B, B), 1)
                first = g[0:B, 0:B] + jnp.where(on, squares[bi][:, 0:B], 0.0)
                second = g[B:, B:] + jnp.where(on, squares[bi][:, B:], 0.0)
                diag = jnp.sum(jnp.where(on, second, 0.0), axis=0, keepdims=True)
                i, j = 2 * bi, 2 * bi + 1
                tile = jnp.concatenate([seg(i), seg(i), seg(j), seg(j), diag, zero, zero, zero], axis=0)
                put(len(LOWER) + bi, jnp.where(lower, first, second), tile)


def local_gram(x, core):
    shape = jax.ShapeDtypeStruct((HALF, ROWS, B), jnp.float32)
    return pl.pallas_call(
        gram_kernel,
        out_shape=(shape, shape),
        in_specs=[SMEM, VMEM],
        out_specs=(VMEM, VMEM),
        scratch_shapes=[pltpu.VMEM(x.shape, jnp.bfloat16)] * 4,
        compiler_params=PARAMS,
    )(core, x)


def merge_kernel(count, a_ref, o_ref):
    sources, rows, _ = a_ref.shape
    block = a_ref[0, 0:B, :]
    for c in range(1, sources):
        block = block + a_ref[c, 0:B, :]
    tiles = [a_ref[c, t : t + 8, :] for c in range(sources) for t in range(B, rows, 8)]
    total = tiles[0]
    for t in tiles[1:]:
        total = total + t
    mean = total * (1.0 / len(tiles))
    sub = iota((8, B), 0)
    left, right = [], []
    square = jnp.zeros((8, B), jnp.float32)
    for t in tiles:
        delta = jnp.where(sub < 4, t - mean, 0.0)
        left.append(delta)
        right.append(jnp.concatenate([delta[1:8], delta[0:1]], axis=0))
        square = square + delta * delta
    left = jnp.concatenate(left, axis=0)
    right = jnp.concatenate(right, axis=0)
    row = iota(left.shape, 0) % 8
    low = dot(jnp.where(row == 0, left, 0.0), jnp.where(row == 0, right, 0.0), (0, 0))
    high = dot(jnp.where(row == 2, left, 0.0), jnp.where(row == 2, right, 0.0), (0, 0))
    lower = iota((B, B), 0) >= iota((B, B), 1)
    block = block + count * jnp.where(lower, low, high)
    diag = total[4:5] + count * square[2:3]
    tile = jnp.where(sub < 4, mean, jnp.where(sub == 4, jnp.broadcast_to(diag, (8, B)), 0.0))
    for c in range(o_ref.shape[0]):
        o_ref[c, 0:B, :] = block
        o_ref[c, B:, :] = tile


def merge(a, count, copies):
    return pl.pallas_call(
        functools.partial(merge_kernel, float(count)),
        out_shape=jax.ShapeDtypeStruct((copies, ROWS, B), jnp.float32),
        in_specs=[VMEM],
        out_specs=VMEM,
        compiler_params=PARAMS,
    )(a)


def join(*parts):
    block = parts[0][:, 0:B]
    for p in parts[1:]:
        block = block + p[:, 0:B]
    return jnp.concatenate([block] + [p[:, B:] for p in parts], axis=1)


def row_of(x, j):
    return jnp.broadcast_to(x[j : j + 1, :], x.shape)


def column_of(x, j):
    return jnp.broadcast_to(x[:, j : j + 1], x.shape)


NEAR = 3


def factor_inverse(rows):
    count = len(rows)
    sub, lane = iota((8, B), 0), iota((8, B), 1)
    for p in range(count):
        own = (lane >= 8 * p) & (lane < 8 * p + 8)
        end = min(count, p + NEAR)
        cols = {q: [column_of(rows[q], 8 * p + j) for j in range(8)] for q in range(p, end)}
        far = jnp.concatenate(rows[end:], axis=0) if end < count else None
        rows[p] = jnp.where(own, (lane - 8 * p == sub).astype(jnp.float32), rows[p])
        for q in range(p + 1, count):
            rows[q] = jnp.where(own, 0.0, rows[q])
        pivots = None
        for j in range(0, 8, 2):
            c = cols[p]
            a, b, d = row_of(c[j], j), row_of(c[j + 1], j), row_of(c[j + 1], j + 1)
            inverse = pl.reciprocal(a, approx=False)
            det = a * d - b * b
            ratio = b * inverse
            second = a * pl.reciprocal(det, approx=False)
            pivots = a if j == 0 else jnp.where(sub == j, a, pivots)
            pivots = jnp.where(sub == j + 1, det * inverse, pivots)
            heads = {m: row_of(c[m], j) for m in range(j + 2, 8)}
            nexts = {m: row_of(c[m], j + 1) - ratio * heads[m] for m in range(j + 2, 8)}
            head = row_of(rows[p], j)
            next_ = row_of(rows[p], j + 1) - ratio * head
            for q in range(p, end):
                k = cols[q]
                u = k[j] * inverse
                v = (k[j + 1] - b * u) * second
                if q == p:
                    u = jnp.where(sub > j, u, 0.0)
                    v = jnp.where(sub > j + 1, v, 0.0)
                for m in range(j + 2, 8):
                    k[m] = k[m] - u * heads[m] - v * nexts[m]
                rows[q] = rows[q] - u * head - v * next_
        root = lax.rsqrt(pivots)
        if end < count:
            inverse = root * root
            y = rows[p] * inverse
            for m in range(7, 0, -1):
                y = y - jnp.where(sub < m, cols[p][m] * inverse, 0.0) * row_of(y, m)
            pad = [jnp.zeros((8 * p, B), jnp.float32)] if p else []
            y = jnp.concatenate(pad + [y, jnp.zeros((B - 8 * p - 8, B), jnp.float32)], axis=0)
            step = dot(far, y, (1, 0))
            for q in range(end, count):
                rows[q] = rows[q] - step[8 * (q - end) : 8 * (q - end) + 8, :]
        rows[p] = rows[p] * root
        yield p


def solve_kernel(scale, core_ref, x_ref, own_ref, other_ref, y_ref, a_ref, z_ref, w_ref, l_ref):
    core = core_ref[0]
    lower = iota((B, B), 0) > iota((B, B), 1)
    equal = iota((B, B), 0) == iota((B, B), 1)
    n, d = x_ref.shape

    def chunk(c, lo, hi):
        mine = core == c // HALF
        return jnp.where(mine, own_ref[c % HALF, lo:hi, :], other_ref[c % HALF, lo:hi, :])

    means = []
    for s in range(len(PAIRS)):
        tile = chunk(len(LOWER) + s, B, ROWS)
        means += [tile[0:1, :], tile[2:3, :]]
    mean = jnp.concatenate(means, axis=1)

    def diagonal(s):
        block = chunk(len(LOWER) + s, 0, B)
        tile = chunk(len(LOWER) + s, B, ROWS)
        low = jnp.where(lower, block, 0.0)
        first = jnp.where(equal, block, low + low.T)
        high = jnp.where(lower | equal, 0.0, block)
        second = jnp.where(equal, jnp.broadcast_to(tile[4:5, :], (B, B)), high + high.T)
        for i, value in ((2 * s, first), (2 * s + 1, second)):
            a_ref[B * i : B * i + B, B * i : B * i + B] = value

    def fill(c, i, j):
        a_ref[B * i : B * i + B, B * j : B * j + B] = chunk(c, 0, B)

    def center(r):
        z_ref[r : r + STEP, :] = (x_ref[r : r + STEP, :] - mean) * scale

    diagonal(0)
    later = [functools.partial(fill, c, i, j) for c, (i, j) in enumerate(LOWER)]
    later += [functools.partial(diagonal, s) for s in range(1, len(PAIRS))]
    later += [functools.partial(center, r) for r in range(0, n, STEP)]
    head = a_ref[0:B, 0:B]
    for k in range(NB):
        lo, hi = B * k, B * k + B
        rows = [head[8 * p : 8 * p + 8, :] for p in range(B // 8)]
        per = -(-len(later) // (B // 8))
        for p in factor_inverse(rows):
            for task in later[per * p : per * p + per]:
                task()
        later = []
        w = jnp.where(lower | equal, jnp.concatenate(rows, axis=0), 0.0)
        if k + 1 < NB:
            near = dot(a_ref[hi : hi + B, lo:hi], w, (1, 1))
            head = a_ref[hi : hi + B, hi : hi + B] - dot(near, near, (1, 1))
            l_ref[k % 2, hi : hi + B, :] = near
            if k + 2 < NB:
                l_ref[k % 2, hi + B : d, :] = dot(a_ref[hi + B : d, lo:hi], w, (1, 1))
        w_ref[k % 2] = w

        def update(j, k=k):
            jl, jh = B * j, B * j + B
            a_ref[jl:d, jl:jh] = a_ref[jl:d, jl:jh] - dot(l_ref[k % 2, jl:d, :], l_ref[k % 2, jl:jh, :], (1, 1))

        def first(k=k):
            jl, jh = B * k + B, B * k + 2 * B
            l = l_ref[k % 2]
            a_ref[jh:d, jl:jh] = a_ref[jh:d, jl:jh] - dot(l[jh:d, :], l[jl:jh, :], (1, 1))

        def solved(r, k=k):
            lo, hi = B * k, B * k + B
            y_ref[r : r + STEP, lo:hi] = dot(z_ref[r : r + STEP, lo:hi], w_ref[k % 2], (1, 1))

        def reduced(r, k=k):
            lo, hi = B * k, B * k + B
            z_ref[r : r + STEP, hi:d] = z_ref[r : r + STEP, hi:d] - dot(
                y_ref[r : r + STEP, lo:hi], l_ref[k % 2, hi:d, :], (1, 1)
            )

        if k + 2 < NB:
            later.append(first)
        later += [functools.partial(update, j) for j in range(k + 2, NB)]
        later += [functools.partial(solved, r) for r in range(0, n, STEP)]
        if k + 1 < NB:
            later += [functools.partial(reduced, r) for r in range(0, n, STEP)]
    for task in later:
        task()


def factor_solve(x, own, other, core, scale):
    return pl.pallas_call(
        functools.partial(solve_kernel, scale),
        out_shape=jax.ShapeDtypeStruct(x.shape, jnp.float32),
        in_specs=[SMEM, VMEM, VMEM, VMEM],
        out_specs=VMEM,
        scratch_shapes=[
            pltpu.VMEM((x.shape[1], x.shape[1]), jnp.float32),
            pltpu.VMEM(x.shape, jnp.float32),
            pltpu.VMEM((2, B, B), jnp.float32),
            pltpu.VMEM((2, x.shape[1], B), jnp.float32),
        ],
        compiler_params=PARAMS,
    )(core, x, own, other)


def z_partner(mask):
    gray = [i ^ (i >> 1) for i in range(8)]
    return [(i, gray.index(g ^ mask)) for i, g in enumerate(gray)]


def per_device(x):
    n = x.shape[0]
    total = n * lax.axis_size("z") * lax.axis_size("core") * lax.axis_size("cols")
    core = jnp.reshape(lax.axis_index("core"), (1,)).astype(jnp.int32)
    swap = [(0, 1), (1, 0)]
    keep, send = local_gram(x, core)
    part = join(keep, lax.ppermute(send, "core", swap))
    part = lax.all_to_all(part, "cols", 0, 0, tiled=True)
    part = merge(part, n, 1)
    part = join(part, lax.ppermute(part, "z", z_partner(1)))
    part = join(part, *[lax.ppermute(part, "z", z_partner(mask)) for mask in (2, 4, 6)])
    copies = merge(part, 2 * n * lax.axis_size("cols"), HALF)
    own = lax.all_to_all(copies, "cols", 0, 0, tiled=True)
    other = lax.ppermute(own, "core", swap)
    return factor_solve(x, own, other, core, math.sqrt(total))


def solution(mesh):
    rows, cols = mesh.devices.shape
    fine = Mesh(mesh.devices.reshape(rows // 2, 2, cols), ("z", "core", "cols"))
    spec = P(("z", "core", "cols"), None)
    return jax.shard_map(per_device, mesh=fine, in_specs=(spec,), out_specs=spec, check_vma=False)
```

```python
import functools
import math

import jax
import jax.numpy as jnp
from jax import lax
from jax.experimental import pallas as pl
from jax.experimental.pallas import tpu as pltpu
from jax.sharding import Mesh, PartitionSpec as P

B = 128
STEP = 256
HIGHEST = lax.Precision.HIGHEST
NB = 8
LOWER = [(i, j) for i in range(NB) for j in range(i)]
PAIRS = [(2 * s, 2 * s + 1) for s in range(NB // 2)]
CHUNKS = len(LOWER) + len(PAIRS)
HALF = CHUNKS // 2
ROWS = B + 8
VMEM = pl.BlockSpec(memory_space=pltpu.VMEM)
HBM = pl.BlockSpec(memory_space=pl.ANY)
SMEM = pl.BlockSpec(memory_space=pltpu.SMEM)
PARAMS = pltpu.CompilerParams(vmem_limit_bytes=56 * 1024 * 1024)


def dot(a, b, dims):
    return lax.dot_general(a, b, ((dims[0:1], dims[1:2]), ((), ())), precision=HIGHEST, preferred_element_type=jnp.float32)


def iota(shape, axis):
    return lax.broadcasted_iota(jnp.int32, shape, axis)


def gram_kernel(core_ref, x_hbm, keep_ref, send_ref, hi_ref, mid_ref, hit_ref, midt_ref, x_ref, sems):
    n, d = x_ref.shape
    wide = 2 * B
    copies = [
        pltpu.make_async_copy(x_hbm.at[:, pl.ds(c, wide)], x_ref.at[:, pl.ds(c, wide)], sems.at[c // wide])
        for c in range(0, d, wide)
    ]
    for copy in copies:
        copy.start()
    means = []
    squares = []

    def prepare(i):
        c = wide * i
        copies[i].wait()
        mean = jnp.sum(x_ref[:, c : c + wide], axis=0, keepdims=True) * (1.0 / n)
        means.append(mean)
        xc = x_ref[:, c : c + wide] - mean
        hi = xc.astype(jnp.bfloat16)
        mid = (xc - hi.astype(jnp.float32)).astype(jnp.bfloat16)
        hi_ref[:, c : c + wide] = hi
        mid_ref[:, c : c + wide] = mid
        low = mid.astype(jnp.float32)
        squares.append(jnp.sum(low * low, axis=0, keepdims=True))
        xt = xc.T
        hi = xt.astype(jnp.bfloat16)
        hit_ref[c : c + wide, :] = hi
        midt_ref[c : c + wide, :] = (xt - hi.astype(jnp.float32)).astype(jnp.bfloat16)

    def product(j):
        total = None
        for a, b in ((hit_ref, hi_ref), (hit_ref, mid_ref), (midt_ref, hi_ref)):
            part = jnp.dot(a[wide * j : d, :], b[:, wide * j : wide * j + wide], preferred_element_type=jnp.float32)
            total = part if total is None else total + part
        return total

    core = core_ref[0]
    lower = iota((B, B), 0) >= iota((B, B), 1)

    def put(chunk, block, tile):
        def write(ref):
            ref[chunk % HALF, 0:B, :] = block
            ref[chunk % HALF, B:, :] = tile

        mine = core == chunk // HALF

        @pl.when(mine)
        def _():
            write(keep_ref)

        @pl.when(jnp.logical_not(mine))
        def _():
            write(send_ref)

    def seg(i):
        return means[i // 2][:, B * (i % 2) : B * (i % 2) + B]

    zero = jnp.zeros((1, B), jnp.float32)
    for bi in range(NB // 2):
        prepare(bi)
    for bj in range(NB // 2):
        panel = product(bj)
        for bi in range(bj, NB // 2):
            g = panel[wide * (bi - bj) : wide * (bi - bj) + wide, :]
            for u in range(2):
                for v in range(2):
                    i, j = 2 * bi + u, 2 * bj + v
                    if i > j:
                        tile = jnp.concatenate([seg(i), seg(j), seg(i), seg(j), zero, zero, zero, zero], axis=0)
                        put(LOWER.index((i, j)), g[B * u : B * u + B, B * v : B * v + B], tile)
            if bi == bj:
                on = iota((B, B), 0) == iota((B, B), 1)
                first = g[0:B, 0:B] + jnp.where(on, squares[bi][:, 0:B], 0.0)
                second = g[B:, B:] + jnp.where(on, squares[bi][:, B:], 0.0)
                diag = jnp.sum(jnp.where(on, second, 0.0), axis=0, keepdims=True)
                i, j = 2 * bi, 2 * bi + 1
                tile = jnp.concatenate([seg(i), seg(i), seg(j), seg(j), diag, zero, zero, zero], axis=0)
                put(len(LOWER) + bi, jnp.where(lower, first, second), tile)


def local_gram(x, core):
    shape = jax.ShapeDtypeStruct((HALF, ROWS, B), jnp.float32)
    return pl.pallas_call(
        gram_kernel,
        out_shape=(shape, shape),
        in_specs=[SMEM, HBM],
        out_specs=(VMEM, VMEM),
        scratch_shapes=[pltpu.VMEM(x.shape, jnp.bfloat16)] * 4
        + [pltpu.VMEM(x.shape, jnp.float32), pltpu.SemaphoreType.DMA((NB // 2,))],
        compiler_params=PARAMS,
    )(core, x)


def merge_kernel(count, a_ref, o_ref):
    sources, rows, _ = a_ref.shape
    block = a_ref[0, 0:B, :]
    for c in range(1, sources):
        block = block + a_ref[c, 0:B, :]
    tiles = [a_ref[c, t : t + 8, :] for c in range(sources) for t in range(B, rows, 8)]
    total = tiles[0]
    for t in tiles[1:]:
        total = total + t
    mean = total * (1.0 / len(tiles))
    sub = iota((8, B), 0)
    left, right = [], []
    square = jnp.zeros((8, B), jnp.float32)
    for t in tiles:
        delta = jnp.where(sub < 4, t - mean, 0.0)
        left.append(delta)
        right.append(jnp.concatenate([delta[1:8], delta[0:1]], axis=0))
        square = square + delta * delta
    left = jnp.concatenate(left, axis=0)
    right = jnp.concatenate(right, axis=0)
    row = iota(left.shape, 0) % 8
    low = dot(jnp.where(row == 0, left, 0.0), jnp.where(row == 0, right, 0.0), (0, 0))
    high = dot(jnp.where(row == 2, left, 0.0), jnp.where(row == 2, right, 0.0), (0, 0))
    lower = iota((B, B), 0) >= iota((B, B), 1)
    block = block + count * jnp.where(lower, low, high)
    diag = total[4:5] + count * square[2:3]
    tile = jnp.where(sub < 4, mean, jnp.where(sub == 4, jnp.broadcast_to(diag, (8, B)), 0.0))
    for c in range(o_ref.shape[0]):
        o_ref[c, 0:B, :] = block
        o_ref[c, B:, :] = tile


def merge(a, count, copies):
    return pl.pallas_call(
        functools.partial(merge_kernel, float(count)),
        out_shape=jax.ShapeDtypeStruct((copies, ROWS, B), jnp.float32),
        in_specs=[VMEM],
        out_specs=VMEM,
        compiler_params=PARAMS,
    )(a)


def join(a, b):
    return jnp.concatenate([a[:, 0:B] + b[:, 0:B], a[:, B:], b[:, B:]], axis=1)


def row_of(x, j):
    return jnp.broadcast_to(x[j : j + 1, :], x.shape)


def column_of(x, j):
    return jnp.broadcast_to(x[:, j : j + 1], x.shape)


def factor_inverse(rows):
    sub, lane = iota((8, B), 0), iota((8, B), 1)
    for p in range(len(rows)):
        own = (lane >= 8 * p) & (lane < 8 * p + 8)
        cols = {q: [column_of(rows[q], 8 * p + j) for j in range(8)] for q in range(p, len(rows))}
        rows[p] = jnp.where(own, (lane - 8 * p == sub).astype(jnp.float32), rows[p])
        for q in range(p + 1, len(rows)):
            rows[q] = jnp.where(own, 0.0, rows[q])
        pivots = None
        for j in range(8):
            pivot = row_of(cols[p][j], j)
            pivots = pivot if j == 0 else jnp.where(sub == j, pivot, pivots)
            inverse = pl.reciprocal(pivot, approx=False)
            heads = {m: row_of(cols[p][m], j) for m in range(j + 1, 8)}
            head = row_of(rows[p], j)
            for q in range(p, len(rows)):
                coef = cols[q][j] * inverse
                if q == p:
                    coef = jnp.where(sub > j, coef, 0.0)
                for m in range(j + 1, 8):
                    cols[q][m] = cols[q][m] - coef * heads[m]
                rows[q] = rows[q] - coef * head
        rows[p] = rows[p] * lax.rsqrt(pivots)
        yield p


def solve_kernel(scale, core_ref, x_hbm, own_ref, other_ref, y_hbm, a_ref, z_ref, w_ref, l_ref, y_ref, in_sem, out_sems):
    core = core_ref[0]
    lower = iota((B, B), 0) > iota((B, B), 1)
    equal = iota((B, B), 0) == iota((B, B), 1)
    x_ref = y_ref
    n, d = x_ref.shape
    load = pltpu.make_async_copy(x_hbm, x_ref, in_sem)
    load.start()
    stores = [
        pltpu.make_async_copy(y_ref.at[:, pl.ds(c, B)], y_hbm.at[:, pl.ds(c, B)], out_sems.at[c // B])
        for c in range(0, d, B)
    ]

    def chunk(c, lo, hi):
        mine = core == c // HALF
        return jnp.where(mine, own_ref[c % HALF, lo:hi, :], other_ref[c % HALF, lo:hi, :])

    means = []
    for s in range(len(PAIRS)):
        tile = chunk(len(LOWER) + s, B, ROWS)
        means += [tile[0:1, :], tile[2:3, :]]
    mean = jnp.concatenate(means, axis=1)

    def diagonal(s):
        block = chunk(len(LOWER) + s, 0, B)
        tile = chunk(len(LOWER) + s, B, ROWS)
        low = jnp.where(lower, block, 0.0)
        first = jnp.where(equal, block, low + low.T)
        high = jnp.where(lower | equal, 0.0, block)
        second = jnp.where(equal, jnp.broadcast_to(tile[4:5, :], (B, B)), high + high.T)
        for i, value in ((2 * s, first), (2 * s + 1, second)):
            a_ref[B * i : B * i + B, B * i : B * i + B] = value

    def fill(c, i, j):
        a_ref[B * i : B * i + B, B * j : B * j + B] = chunk(c, 0, B)

    def center(r):
        z_ref[r : r + STEP, :] = (x_ref[r : r + STEP, :] - mean) * scale

    diagonal(0)
    later = [functools.partial(fill, c, i, j) for c, (i, j) in enumerate(LOWER)]
    later += [functools.partial(diagonal, s) for s in range(1, len(PAIRS))]
    later.append(load.wait)
    later += [functools.partial(center, r) for r in range(0, n, STEP)]
    head = a_ref[0:B, 0:B]
    for k in range(NB):
        lo, hi = B * k, B * k + B
        rows = [head[8 * p : 8 * p + 8, :] for p in range(B // 8)]
        per = -(-len(later) // (B // 8))
        for p in factor_inverse(rows):
            for task in later[per * p : per * p + per]:
                task()
        later = []
        w = jnp.where(lower | equal, jnp.concatenate(rows, axis=0), 0.0)
        if k + 1 < NB:
            near = dot(a_ref[hi : hi + B, lo:hi], w, (1, 1))
            head = a_ref[hi : hi + B, hi : hi + B] - dot(near, near, (1, 1))
            l_ref[k % 2, hi : hi + B, :] = near
            if k + 2 < NB:
                l_ref[k % 2, hi + B : d, :] = dot(a_ref[hi + B : d, lo:hi], w, (1, 1))
        w_ref[k % 2] = w

        def update(j, k=k):
            jl, jh = B * j, B * j + B
            a_ref[jl:d, jl:jh] = a_ref[jl:d, jl:jh] - dot(l_ref[k % 2, jl:d, :], l_ref[k % 2, jl:jh, :], (1, 1))

        def first(k=k):
            jl, jh = B * k + B, B * k + 2 * B
            l = l_ref[k % 2]
            a_ref[jh:d, jl:jh] = a_ref[jh:d, jl:jh] - dot(l[jh:d, :], l[jl:jh, :], (1, 1))

        def solved(r, k=k):
            lo, hi = B * k, B * k + B
            y_ref[r : r + STEP, lo:hi] = dot(z_ref[r : r + STEP, lo:hi], w_ref[k % 2], (1, 1))

        def reduced(r, k=k):
            lo, hi = B * k, B * k + B
            z_ref[r : r + STEP, hi:d] = z_ref[r : r + STEP, hi:d] - dot(
                y_ref[r : r + STEP, lo:hi], l_ref[k % 2, hi:d, :], (1, 1)
            )

        if k + 2 < NB:
            later.append(first)
        later += [functools.partial(update, j) for j in range(k + 2, NB)]
        later += [functools.partial(solved, r) for r in range(0, n, STEP)]
        later.append(stores[k].start)
        if k + 1 < NB:
            later += [functools.partial(reduced, r) for r in range(0, n, STEP)]
    for task in later:
        task()
    for store in stores:
        store.wait()


def factor_solve(x, own, other, core, scale):
    return pl.pallas_call(
        functools.partial(solve_kernel, scale),
        out_shape=jax.ShapeDtypeStruct(x.shape, jnp.float32),
        in_specs=[SMEM, HBM, VMEM, VMEM],
        out_specs=HBM,
        scratch_shapes=[
            pltpu.VMEM((x.shape[1], x.shape[1]), jnp.float32),
            pltpu.VMEM(x.shape, jnp.float32),
            pltpu.VMEM((2, B, B), jnp.float32),
            pltpu.VMEM((2, x.shape[1], B), jnp.float32),
            pltpu.VMEM(x.shape, jnp.float32),
            pltpu.SemaphoreType.DMA(()),
            pltpu.SemaphoreType.DMA((NB,)),
        ],
        compiler_params=PARAMS,
    )(core, x, own, other)


def z_steps():
    gray = [i ^ (i >> 1) for i in range(8)]
    place = {g: i for i, g in enumerate(gray)}
    return [[(i, place[gray[i] ^ (1 << k)]) for i in range(8)] for k in range(3)]


def per_device(x):
    n = x.shape[0]
    total = n * lax.axis_size("z") * lax.axis_size("core") * lax.axis_size("cols")
    core = jnp.reshape(lax.axis_index("core"), (1,)).astype(jnp.int32)
    swap = [(0, 1), (1, 0)]
    keep, send = local_gram(x, core)
    part = join(keep, lax.ppermute(send, "core", swap))
    part = lax.all_to_all(part, "cols", 0, 0, tiled=True)
    part = merge(part, n, 1)
    for step in z_steps():
        part = join(part, lax.ppermute(part, "z", step))
    copies = merge(part, 2 * n * lax.axis_size("cols"), HALF)
    own = lax.all_to_all(copies, "cols", 0, 0, tiled=True)
    other = lax.ppermute(own, "core", swap)
    return factor_solve(x, own, other, core, math.sqrt(total))


def solution(mesh):
    rows, cols = mesh.devices.shape
    fine = Mesh(mesh.devices.reshape(rows // 2, 2, cols), ("z", "core", "cols"))
    spec = P(("z", "core", "cols"), None)
    return jax.shard_map(per_device, mesh=fine, in_specs=(spec,), out_specs=spec, check_vma=False)
```
